256 devices in a mesh: node: 16 (over z, core), local: 16 (over y, x).
Axes of the slice: x: 4, y: 4, z: 8, core: 2. Of those that a mesh axis runs over, the one named last changes fastest.
Arguments:
- tokens: bfloat16 [2048, 7168], P(('node', 'local')), may hold values from -6 to 6
- expert_ids: int32 [2048, 2], P(('node', 'local')), may hold values from 0 to 15, all different within a row; in each aligned block of 8 rows (0 to 7, 8 to 15, ...) at most 2 rows name the same one
- gate_scales: float32 [2048, 2], P(('node', 'local')), may hold values from 0.2 to 1.5
- placement: int32 [16], replicated, may hold values from 0 to 15, each once
- expert_gate: bfloat16 [16, 7168, 2048], P('node', None, 'local'), may hold values from -0.0625 to 0.0625
- expert_up: bfloat16 [16, 7168, 2048], P('node', None, 'local'), may hold values from -0.0625 to 0.0625
- expert_down: bfloat16 [16, 2048, 7168], P('node', 'local'), may hold values from -0.125 to 0.125
- shared_gate: bfloat16 [7168, 2048], P(None, 'local'), may hold values from -0.0625 to 0.0625
- shared_up: bfloat16 [7168, 2048], P(None, 'local'), may hold values from -0.0625 to 0.0625
- shared_down: bfloat16 [2048, 7168], P('local'), may hold values from -0.125 to 0.125
Outputs:
- mixed: bfloat16 [2048, 7168], P(('node', 'local'))
The draws below stay inside these ranges and needn't reach their ends.
Inputs may be any that keep to these rules, and one draw needn't show every extreme that they name: `expert_ids`: each token names 2 different experts; among the rows of one device no expert is named more than 2 times, and that many is reached. `placement`: every node holds exactly one expert.
All inputs are finite; a program needn't handle non-finite values.
Results may differ from the reference program's by a relative error of at most 0.019.
Values may be sent and summed in bfloat16 or wider, within the bound.
No kernel may reach another device: no remote copies, remote signals or barrier semaphores. Data moves between devices by JAX's collectives and lax.ppermute only.
A program may use at most 128 MiB of HBM per device.

```python
import math
from functools import partial
import jax
import jax.numpy as jnp
import numpy as np
from jax import lax

D = 7168
FF = 2048
TOK_DEV = 8
SLOTS = 2
EXPERTS = 16
CAP = 2
TOKENS = 2048
N_NODE = 16
N_LOCAL = 16


def block_scale(rng, extent, shards, least, largest):
    level, own = 1.0, jax.random.fold_in(rng, 6)
    for dim, shards_of in shards:
        steps = jnp.exp(jax.random.uniform(jax.random.fold_in(own, dim), (shards_of,), jnp.float32, least / len(shards), largest / len(shards)))
        level = level * jnp.repeat(steps, extent[dim] // shards_of).reshape([-1 if axis == dim else 1 for axis in range(len(extent))])
    return level


def assign_block(own_key, own, number, rows, amount, top, bound, lean):
    sequence = jax.random.permutation(own_key, amount)
    heavy_load, usual = portions_of(amount, rows * top, bound, lean, True), portions_of(amount, rows * top, bound, lean, False)
    places = jnp.arange(amount)

    def named(sizes, rotation):
        used = int((sizes > 0).sum())
        fixed = max(1, used // 4)
        moved = fixed + (places - fixed + rotation * (used - fixed)) % max(1, amount - fixed)
        return jnp.zeros((amount,), jnp.int32).at[sequence[jnp.where(places < fixed, places, moved)]].set(jnp.asarray(sizes, jnp.int32))

    sizes = jnp.where(number % 4 == 0, named(heavy_load, number // 4), named(usual, number - number // 4 - 1))
    mixed = jax.random.permutation(jax.random.fold_in(own, 3), amount)
    source_of, receiver = mixed[0:amount // 2 * 2:2], mixed[1:amount // 2 * 2:2]
    margin = jnp.minimum(sizes[source_of] - 1, bound - sizes[receiver]) // 2
    margin = jnp.where((source_of == sequence[0]) | (receiver == sequence[0]) | (sizes[receiver] == 0), 0, jnp.maximum(margin, 0))
    moved = jax.random.randint(jax.random.fold_in(own, 4), (amount // 2,), 0, 1 << 20) % (margin + 1)
    sizes = sizes.at[source_of].add(-moved).at[receiver].add(moved)
    items = jnp.searchsorted(jnp.cumsum(sizes), jnp.arange(rows * top), side="right").astype(jnp.int32)
    table = items.reshape(top, rows).T
    table = table[jax.random.permutation(jax.random.fold_in(own, 1), rows)]
    rotation = jax.random.randint(jax.random.fold_in(own, 2), (rows, 1), 0, top)
    return jnp.take_along_axis(table, (jnp.arange(top)[None, :] + rotation) % top, axis=1)


def portions_of(amount, total, bound, skew, full):
    weights = [(1 << 20) // math.isqrt(standing ** skew) + 1 for standing in range(1, amount + 1)]
    largest = bound if full else min(bound, max(-(-total // amount), total * weights[0] // sum(weights)))
    least = 1 if total - largest >= amount - 1 else 0
    holding, spare = [largest] + [least] * (amount - 1), total - largest - least * (amount - 1)
    while spare > 0:
        movable = [i for i in range(1, amount) if holding[i] < largest] or [i for i in range(1, amount) if holding[i] < bound]
        whole, left = sum([weights[i] for i in movable]), spare
        for i in movable:
            extra = min(bound - holding[i], max(1, left * weights[i] // whole), spare)
            holding[i] = holding[i] + extra
            spare = spare - extra
    return np.array(holding)


def scatter_about(rng, dims, deviation, reach, split=(), held_as=jnp.bfloat16):
    array = deviation * jax.random.normal(rng, dims, jnp.float32)
    if split:
        array = array * block_scale(rng, dims, split, -0.22, 0.18)
    return jnp.clip(array, -reach, reach).astype(held_as)


def setup_inputs(seed: int = 0) -> dict:
    seeds = jax.random.split(jax.random.key(seed), 11)
    tokens = scatter_about(seeds[0], (TOKENS, D), 1.0, 6.0, ((0, 256),))
    expert_ids_keys = jax.random.split(jax.random.fold_in(seeds[1], 1), TOKENS // TOK_DEV)
    expert_ids_turns = jax.random.permutation(jax.random.fold_in(seeds[1], 3), TOKENS // TOK_DEV)
    expert_ids = jax.vmap(lambda own, number: assign_block(jax.random.fold_in(seeds[1], 2), own, number, TOK_DEV, EXPERTS, SLOTS, CAP, 2))(expert_ids_keys, expert_ids_turns).reshape((TOKENS, SLOTS))
    gate_scales = jnp.clip(0.2 + 1.3 * jax.random.uniform(seeds[2], (TOKENS, SLOTS), jnp.float32) ** block_scale(seeds[2], (TOKENS, SLOTS), ((0, 256),), -0.2, 0.2), 0.2, 1.5)
    placement = jax.random.permutation(seeds[3], EXPERTS).astype(jnp.int32)
    expert_gate = scatter_about(seeds[4], (EXPERTS, D, FF), D ** -0.5, 0.0625, ((0, 16), (2, 16)))
    expert_up = scatter_about(seeds[5], (EXPERTS, D, FF), D ** -0.5, 0.0625, ((0, 16), (2, 16)))
    expert_down = scatter_about(seeds[6], (EXPERTS, FF, D), FF ** -0.5, 0.125, ((0, 16), (1, 16)))
    shared_gate = scatter_about(seeds[7], (D, FF), D ** -0.5, 0.0625, ((1, 16),))
    shared_up = scatter_about(seeds[8], (D, FF), D ** -0.5, 0.0625, ((1, 16),))
    shared_down = scatter_about(seeds[9], (FF, D), FF ** -0.5, 0.125, ((0, 16),))
    return {"tokens": tokens, "expert_ids": expert_ids, "gate_scales": gate_scales, "placement": placement, "expert_gate": expert_gate, "expert_up": expert_up, "expert_down": expert_down, "shared_gate": shared_gate, "shared_up": shared_up, "shared_down": shared_down}


def destinations(expert_ids, placement):
    labels = jnp.arange(placement.shape[0], dtype=jnp.int32)
    matches = expert_ids[..., None] == labels
    return jnp.sum(jnp.where(matches, placement, 0), axis=-1).astype(jnp.int32)


def slot_index(targets, capacity, node_count):
    labels = jnp.arange(node_count, dtype=jnp.int32)
    marks = (targets[:, None] == labels[None, :]).astype(jnp.int32)
    earlier = jnp.cumsum(marks, axis=0) - marks
    position = jnp.sum(earlier * marks, axis=1)
    return (targets * capacity + position).astype(jnp.int32)


def combine(own_slots, gate_scales, outputs, tok_rows, slot_count):
    labels = jnp.arange(outputs.shape[0], dtype=jnp.int32)
    scales = gate_scales.reshape(-1)[:, None].astype(jnp.float32)
    weights = jnp.where(own_slots[:, None] == labels[None, :], scales, jnp.float32(0.0))
    weights = jnp.sum(weights.reshape(tok_rows, slot_count, -1), axis=1)
    return jnp.dot(weights, outputs.astype(jnp.float32), precision=lax.Precision.HIGHEST)


def expert_sum(token_rows, gate_weight, up_weight, down_weight, groups):
    gate = jnp.dot(token_rows, gate_weight, preferred_element_type=jnp.float32)
    lifted = jnp.dot(token_rows, up_weight, preferred_element_type=jnp.float32)
    hidden = (jax.nn.silu(gate) * lifted).astype(jnp.bfloat16)
    group_width = down_weight.shape[0] // groups

    def add_group(index, total):
        start = (index * group_width).astype(jnp.int32)
        hidden_part = lax.dynamic_slice_in_dim(hidden, start, group_width, 1)
        down_part = lax.dynamic_slice_in_dim(down_weight, start, group_width, 0)
        term = jnp.dot(hidden_part, down_part, preferred_element_type=jnp.float32).astype(jnp.bfloat16)
        term = lax.optimization_barrier(term)
        return total + term.astype(jnp.float32)

    initial = jnp.zeros((token_rows.shape[0], down_weight.shape[1]), jnp.float32)
    return lax.fori_loop(0, groups, add_group, initial)


def reference(tokens, expert_ids, gate_scales, placement, expert_gate, expert_up, expert_down, shared_gate, shared_up, shared_down):
    devices = N_NODE * N_LOCAL
    tok_blocks = tokens.reshape(devices, TOK_DEV, D)
    id_blocks = expert_ids.reshape(devices, TOK_DEV, SLOTS)
    scale_blocks = gate_scales.reshape(devices, TOK_DEV, SLOTS)

    def dispatch(block_tokens, block_ids):
        targets = destinations(block_ids, placement).reshape(-1)
        slots = slot_index(targets, CAP, EXPERTS)
        labels = jnp.arange(EXPERTS * CAP, dtype=jnp.int32)
        table = (labels[:, None] == slots[None, :]).astype(jnp.bfloat16)
        repeated = jnp.repeat(block_tokens, SLOTS, axis=0)
        filled = jnp.dot(table, repeated, preferred_element_type=jnp.float32).astype(jnp.bfloat16)
        return filled.reshape(EXPERTS, CAP, D), slots

    buffers, all_slots = jax.vmap(dispatch)(tok_blocks, id_blocks)

    def run_expert(holder):
        expert_rows = buffers[:, holder].reshape(devices * CAP, D)
        result = expert_sum(expert_rows, expert_gate[holder], expert_up[holder], expert_down[holder], N_LOCAL)
        return result.reshape(devices, CAP, D)

    outputs = lax.map(run_expert, jnp.arange(EXPERTS, dtype=jnp.int32))
    per_device = jnp.swapaxes(outputs, 0, 1).reshape(devices, EXPERTS * CAP, D)
    shared_out = expert_sum(tokens, shared_gate, shared_up, shared_down, N_LOCAL)
    routed = jax.vmap(partial(combine, tok_rows=TOK_DEV, slot_count=SLOTS))(all_slots, scale_blocks, per_device)
    return (shared_out + routed.reshape(TOKENS, D)).astype(jnp.bfloat16)
```

```python
import jax
import jax.numpy as jnp
from jax import lax
from jax.experimental import pallas as pl
from jax.experimental.pallas import tpu as pltpu
from jax.sharding import PartitionSpec as P

SIDE = 4
OFFS = (0, 1, -1, 2)
BF16, F32 = jnp.bfloat16, jnp.float32


def move(value, axis, step):
    pairs = []
    for y in range(SIDE):
        for x in range(SIDE):
            ty, tx = ((y + step) % SIDE, x) if axis == 0 else (y, (x + step) % SIDE)
            pairs.append((y * SIDE + x, ty * SIDE + tx))
    return lax.ppermute(value, "local", pairs)


def gather_ring(block, axis):
    half = block.shape[-1] // 2
    ahead = move(block, axis, -1)
    behind = move(block, axis, 1)
    left = move(ahead[:, :half], axis, -1)
    right = move(behind[:, half:], axis, 1)
    return block, ahead, behind, left, right


def scatter_ring(own, ahead, behind, left, right, axis):
    half = own.shape[-1] // 2
    from_behind = move(left, axis, 1)
    from_ahead = move(right, axis, -1)
    ahead = ahead.astype(F32) + jnp.pad(from_behind.astype(F32), ((0, 0), (0, half)))
    behind = behind.astype(F32) + jnp.pad(from_ahead.astype(F32), ((0, 0), (half, 0)))
    got_one = move(ahead.astype(BF16), axis, 1)
    got_two = move(behind.astype(BF16), axis, -1)
    return own.astype(F32) + got_one.astype(F32) + got_two.astype(F32)


def group(blocks, routed):
    return jnp.concatenate([b[:routed] for b in blocks] + [b[routed:] for b in blocks], axis=0)


def ungroup(stack, index, routed, own):
    base = SIDE * routed
    return jnp.concatenate(
        [stack[index * routed : (index + 1) * routed], stack[base + index * own : base + (index + 1) * own]], axis=0
    )


def mlp_kernel(routed, own, *refs):
    a_in, b_in = refs[0:5], refs[5:10]
    eg, eu, ed, sg, su, sd = refs[10:16]
    a_out, b_out = refs[16:21], refs[21:26]
    acc_e, acc_s, hid_e, hid_s = refs[26:30]
    width = a_in[0].shape[1]
    half = width // 2
    rows_e, rows_s = SIDE * routed, SIDE * own

    def product(parts, rows, weight, base):
        if len(parts) == 1:
            return jnp.dot(parts[0][rows, :], weight[pl.ds(base, width), :], preferred_element_type=F32)
        one = jnp.dot(parts[0][rows, :], weight[pl.ds(base, half), :], preferred_element_type=F32)
        two = jnp.dot(parts[1][rows, :], weight[pl.ds(base + half, half), :], preferred_element_type=F32)
        return one + two

    erows, srows = pl.ds(0, rows_e), pl.ds(rows_e, rows_s)
    for i in range(SIDE):
        parts = a_in[3:5] if i == 3 else a_in[i : i + 1]
        for k, weight in enumerate((eg, eu)):
            acc_e[k, i] = product(parts, erows, weight, 0)
        for k, weight in enumerate((sg, su)):
            acc_s[k, i] = product(parts, srows, weight, 0)
    for j in range(SIDE):
        parts = b_in[3:5] if j == 3 else b_in[j : j + 1]
        for k, weight in enumerate((eg, eu)):
            got = product(parts, erows, weight, width)
            for i in range(SIDE):
                acc_e[k, i, j * routed : (j + 1) * routed] += got[i * routed : (i + 1) * routed]
        for k, weight in enumerate((sg, su)):
            got = product(parts, srows, weight, width)
            for i in range(SIDE):
                acc_s[k, i, j * own : (j + 1) * own] += got[i * own : (i + 1) * own]
    for i in range(SIDE):
        gate = acc_e[0, i]
        acc_e[0, i] = gate / (1.0 + jnp.exp(-gate)) * acc_e[1, i]
        gate = acc_s[0, i]
        acc_s[0, i] = gate / (1.0 + jnp.exp(-gate)) * acc_s[1, i]
    for i in range(SIDE):
        for j in range(SIDE):
            hid_e[j, i * routed : (i + 1) * routed] = acc_e[0, i, j * routed : (j + 1) * routed]
            hid_s[j, i * own : (i + 1) * own] = acc_s[0, i, j * own : (j + 1) * own]

    step = 256
    for outs, base, get_e, get_s in (
        (a_out, 0, lambda i: acc_e[0, i], lambda i: acc_s[0, i]),
        (b_out, width, lambda i: hid_e[i], lambda i: hid_s[i]),
    ):
        for i in range(SIDE):
            he, hs = get_e(i).astype(BF16), get_s(i).astype(BF16)
            targets = ((outs[3], 0), (outs[4], half)) if i == 3 else ((outs[i], 0),)
            for out, start in targets:

                @pl.loop(0, out.shape[1] // step)
                def _(c, out=out, start=start, he=he, hs=hs):
                    at = pl.multiple_of(c * step, step)
                    columns = pl.ds(pl.multiple_of(base + start + at, step), step)
                    out[0:rows_e, pl.ds(at, step)] = jnp.dot(he, ed[:, columns], preferred_element_type=F32).astype(BF16)
                    out[rows_e : rows_e + rows_s, pl.ds(at, step)] = jnp.dot(
                        hs, sd[:, columns], preferred_element_type=F32
                    ).astype(BF16)


def mlp(a_parts, b_parts, weights, routed, own):
    group_width = weights[0].shape[1]
    shapes = [jax.ShapeDtypeStruct(p.shape, BF16) for p in (*a_parts, *b_parts)]
    rows = a_parts[0].shape[0]
    features = weights[0].shape[0]
    return pl.pallas_call(
        lambda *refs: mlp_kernel(routed, own, *refs),
        out_shape=shapes,
        in_specs=[pl.BlockSpec(memory_space=pltpu.VMEM)] * 16,
        out_specs=[pl.BlockSpec(memory_space=pltpu.VMEM)] * 10,
        scratch_shapes=[
            pltpu.VMEM((2, SIDE, SIDE * routed, group_width), F32),
            pltpu.VMEM((2, SIDE, SIDE * own, group_width), F32),
            pltpu.VMEM((SIDE, SIDE * routed, group_width), F32),
            pltpu.VMEM((SIDE, SIDE * own, group_width), F32),
        ],
        compiler_params=pltpu.CompilerParams(vmem_limit_bytes=48 * 1024 * 1024),
        cost_estimate=pl.CostEstimate(
            flops=2 * 3 * SIDE * rows * features * group_width,
            bytes_accessed=2 * (2 * SIDE * rows * features + 6 * features * group_width),
            transcendentals=SIDE * rows * group_width,
        ),
    )(*a_parts, *b_parts, *weights)


def per_device(
    tokens, expert_ids, gate_scales, placement, expert_gate, expert_up, expert_down, shared_gate, shared_up, shared_down
):
    node_count = lax.axis_size("node")
    own, features = tokens.shape
    capacity = 2
    routed = node_count * capacity
    half = features // 2

    ids = expert_ids.reshape(-1)
    labels = jnp.arange(node_count, dtype=jnp.int32)
    targets = jnp.sum(jnp.where(ids[:, None] == labels, placement, 0), axis=-1)
    order = jnp.arange(ids.shape[0], dtype=jnp.int32)
    earlier = (targets[:, None] == targets[None, :]) & (order[None, :] < order[:, None])
    slots = targets * capacity + jnp.sum(earlier.astype(jnp.int32), axis=1)
    slots = slots.reshape(own, -1)
    rows = jnp.arange(routed, dtype=jnp.int32)
    marks = slots[:, :, None] == rows

    table = jnp.sum(marks.astype(F32), axis=1).astype(BF16)
    blocks = lax.dot_general(table, tokens, (((0,), (0,)), ((), ())), preferred_element_type=F32).astype(BF16)
    arrived = lax.all_to_all(
        blocks.reshape(node_count, capacity, features), "node", split_axis=0, concat_axis=0, tiled=True
    ).reshape(routed, features)
    load = jnp.concatenate([arrived, tokens], axis=0)

    def spread(value, first):
        near = gather_ring(value, first)
        four = (*near[:3], jnp.concatenate(near[3:], axis=1))
        return gather_ring(group(four, routed), 1 - first)

    a_parts = spread(load[:, :half], 1)
    b_parts = spread(load[:, half:], 0)
    weights = (expert_gate[0], expert_up[0], expert_down[0], shared_gate, shared_up, shared_down)
    outs = mlp(a_parts, b_parts, weights, routed, own)

    def collect(parts, first):
        four = scatter_ring(*parts, 1 - first).astype(BF16)
        blocks = [ungroup(four, i, routed, own) for i in range(SIDE)]
        quarter = half // 2
        return scatter_ring(*blocks[:3], blocks[3][:, :quarter], blocks[3][:, quarter:], first)

    summed = jnp.concatenate([collect(outs[:5], 1), collect(outs[5:], 0)], axis=1)
    back = lax.all_to_all(
        summed[:routed].astype(BF16).reshape(node_count, capacity, features),
        "node",
        split_axis=0,
        concat_axis=0,
        tiled=True,
    ).reshape(routed, features)
    scales = jnp.sum(jnp.where(marks, gate_scales[:, :, None], jnp.float32(0.0)), axis=1)
    mixed = summed[routed:] + jnp.dot(scales, back.astype(F32), precision=lax.Precision.HIGHEST)
    return mixed.astype(BF16)


def solution(mesh):
    placed = (
        P(("node", "local"), None),
        P(("node", "local"), None),
        P(("node", "local"), None),
        P(),
        P("node", None, "local"),
        P("node", None, "local"),
        P("node", "local", None),
        P(None, "local"),
        P(None, "local"),
        P("local", None),
    )
    return jax.shard_map(
        per_device, mesh=mesh, in_specs=placed, out_specs=P(("node", "local"), None), check_vma=False
    )
```

```python
import jax
import jax.numpy as jnp
from jax import lax
from jax.experimental import pallas as pl
from jax.experimental.pallas import tpu as pltpu
from jax.sharding import PartitionSpec as P

SIDE = 4
CAPACITY = 2
AUX = 128
BF16, F32 = jnp.bfloat16, jnp.float32


def move(value, axis, step):
    pairs = []
    for y in range(SIDE):
        for x in range(SIDE):
            ty, tx = ((y + step) % SIDE, x) if axis == 0 else (y, (x + step) % SIDE)
            pairs.append((y * SIDE + x, ty * SIDE + tx))
    return lax.ppermute(value, "local", pairs)


def gather_direct(block, axis):
    return [block, move(block, axis, -1), move(block, axis, 1), move(block, axis, 2)]


def scatter_direct(terms, axis):
    got = [move(terms[1], axis, 1), move(terms[2], axis, -1), move(terms[3], axis, 2)]
    return sum((g.astype(F32) for g in got), terms[0].astype(F32))


def call(kernel, outs, scratch, cost, *args):
    return pl.pallas_call(
        kernel,
        out_shape=outs,
        in_specs=[pl.BlockSpec(memory_space=pltpu.VMEM)] * len(args),
        out_specs=[pl.BlockSpec(memory_space=pltpu.VMEM)] * len(outs),
        scratch_shapes=scratch,
        compiler_params=pltpu.CompilerParams(vmem_limit_bytes=28 * 1024 * 1024),
        cost_estimate=cost,
    )(*args)


def dispatch_kernel(ids, scales, placement, tokens, blocks, pick):
    own, features = tokens.shape
    nodes, routed = placement.shape[1], blocks.shape[0]
    lanes = AUX
    label = lax.broadcasted_iota(jnp.int32, (own, nodes), 1)
    hits, counts = [], jnp.zeros((own, nodes), F32)
    for k in range(ids.shape[1]):
        target = jnp.sum(jnp.where(ids[:, k : k + 1] == label, placement[...], 0), axis=1, keepdims=True)
        hits.append((target, jnp.where(target == label, 1.0, 0.0)))
        counts += hits[-1][1]
    before = jnp.where(
        lax.broadcasted_iota(jnp.int32, (own, own), 0) > lax.broadcasted_iota(jnp.int32, (own, own), 1), 1.0, 0.0
    )
    earlier = jnp.dot(before, counts, preferred_element_type=F32)
    row = lax.broadcasted_iota(jnp.int32, (own, lanes), 1)
    table, aux = jnp.zeros((own, lanes), F32), jnp.zeros((lanes, lanes), F32)
    for k, (target, hit) in enumerate(hits):
        position = jnp.sum(earlier * hit, axis=1, keepdims=True).astype(jnp.int32)
        mark = jnp.where(target * CAPACITY + position == row, 1.0, 0.0)
        scale = scales[:, k : k + 1]
        high = scale.astype(BF16).astype(F32)
        middle = (scale - high).astype(BF16).astype(F32)
        low = (scale - high - middle).astype(BF16).astype(F32)
        beside = jnp.where(row == 0, high, jnp.where(row == 1, middle, jnp.where(row == 2, low, 0.0)))
        if k == 0:
            beside = jnp.where(row == 3, 1.0, beside)
        table += mark
        aux += jnp.dot(mark.T.astype(BF16), beside.astype(BF16), preferred_element_type=F32)
    pick[...] = table
    spread = table.T[:routed].astype(BF16)
    blocks[:, 0:features] = jnp.dot(spread, tokens[...], preferred_element_type=F32).astype(BF16)
    blocks[:, features : features + AUX] = aux[:routed].astype(BF16)


def dispatch(ids, scales, placement, tokens):
    own, features = tokens.shape
    routed = placement.shape[0] * CAPACITY
    return call(
        dispatch_kernel,
        [jax.ShapeDtypeStruct((routed, features + AUX), BF16), jax.ShapeDtypeStruct((own, AUX), F32)],
        [],
        pl.CostEstimate(flops=2 * own * routed * features, bytes_accessed=4 * routed * features, transcendentals=0),
        ids,
        scales,
        placement.reshape(1, -1),
        tokens,
    )


def mlp_kernel(pieces, *refs):
    count = sum(pieces)
    ins, weights, outs = refs[:count], refs[count : count + 6], refs[count + 6 : 2 * count + 6]
    acc = refs[2 * count + 6]
    gate, up, down, shared_gate, shared_up, shared_down = weights
    features, width = gate.shape
    places, at = [], 0
    for parts in pieces:
        places.append(range(at, at + parts))
        at += parts
    rows = [ins[p[0]].shape[0] for p in places]

    def read(base, size):
        values = []
        for p in places:
            first = outs[p[0]].shape[1]
            which = min(base // first, len(p) - 1)
            values.append(ins[p[which]][:, pl.ds(base - which * first, size)])
        return jnp.concatenate(values, axis=0)

    chunk = 1792
    for base in range(0, features, chunk):
        x = read(base, chunk)
        for k, (one, two) in enumerate(((gate, up), (shared_gate, shared_up))):
            weight = jnp.concatenate([one[pl.ds(base, chunk), :], two[pl.ds(base, chunk), :]], axis=1)
            got = jnp.dot(x, weight, preferred_element_type=F32)
            acc[k] = got if base == 0 else acc[k] + got
    aux = read(features, AUX).astype(F32)
    factors = (aux[:, 0:1] + aux[:, 1:2] + aux[:, 2:3], aux[:, 3:4])
    hidden = []
    for k, factor in enumerate(factors):
        g = acc[k, :, :width]
        hidden.append((g / (1.0 + jnp.exp(-g)) * acc[k, :, width:] * factor).astype(BF16))
    hidden = jnp.concatenate(hidden, axis=1)

    step = 512
    shortest = min(o.shape[1] for o in outs)

    for start in range(0, features, shortest):

        @pl.loop(0, shortest // step)
        def _(c):
            at = pl.multiple_of(c * step, step)
            columns = pl.ds(start + at, step)
            weight = jnp.concatenate([down[:, columns], shared_down[:, columns]], axis=0)
            got = jnp.dot(hidden, weight, preferred_element_type=F32).astype(BF16)
            first = 0
            for p, n in zip(places, rows, strict=True):
                size = outs[p[0]].shape[1]
                outs[p[start // size]][:, pl.ds(start % size + at, step)] = got[first : first + n]
                first += n


def mlp(pieces, weights):
    flat = [a for p in pieces for a in p]
    counts = [len(p) for p in pieces]
    rows = sum(p[0].shape[0] for p in pieces)
    features, width = weights[0].shape
    outs = call(
        lambda *refs: mlp_kernel(counts, *refs),
        [jax.ShapeDtypeStruct((p[0].shape[0], features // len(p)), BF16) for p in pieces for _ in p],
        [pltpu.VMEM((2, rows, 2 * width), F32)],
        pl.CostEstimate(
            flops=2 * 6 * rows * features * width,
            bytes_accessed=2 * (2 * rows * features + 6 * features * width),
            transcendentals=2 * rows * width,
        ),
        *flat,
        *weights,
    )
    split, at = [], 0
    for n in counts:
        split.append(outs[at : at + n])
        at += n
    return split


def per_device(
    tokens, expert_ids, gate_scales, placement, expert_gate, expert_up, expert_down, shared_gate, shared_up, shared_down
):
    nodes = lax.axis_size("node")
    features = tokens.shape[1]
    routed = nodes * CAPACITY
    half = features // 2
    weights = (expert_gate[0], expert_up[0], expert_down[0], shared_gate, shared_up, shared_down)
    hold = lax.optimization_barrier

    blocks, pick = dispatch(expert_ids, gate_scales, placement, tokens)
    arrived = lax.all_to_all(
        blocks.reshape(nodes, CAPACITY, -1), "node", split_axis=0, concat_axis=0, tiled=True
    ).reshape(routed, -1)

    firsts, seconds = (1, 0), (0, 1)
    sets = [
        jnp.concatenate(gather_direct(part, a), axis=0)
        for part, a in zip((arrived[: routed // 2], arrived[routed // 2 :]), firsts, strict=True)
    ]
    sets = hold(sets)
    ahead = [move(s, a, -1) for s, a in zip(sets, seconds, strict=True)]
    behind = [move(s, a, 1) for s, a in zip(sets, seconds, strict=True)]
    out_own = mlp([[s] for s in sets], weights)
    ahead, behind, out_own = hold((ahead, behind, out_own))
    left = [move(s[:, :half], a, -1) for s, a in zip(ahead, seconds, strict=True)]
    right = [move(s[:, half:], a, 1) for s, a in zip(behind, seconds, strict=True)]
    out_near = mlp([[s] for s in (*ahead, *behind)], weights)
    left, right, out_near = hold((left, right, out_near))
    out_far = mlp([[p, q] for p, q in zip(left, right, strict=True)], weights)

    from_behind = [move(o[0], a, 1) for o, a in zip(out_far, seconds, strict=True)]
    from_ahead = [move(o[1], a, -1) for o, a in zip(out_far, seconds, strict=True)]
    from_behind, from_ahead = hold((from_behind, from_ahead))
    one, two = [], []
    for k, a in enumerate(seconds):
        term = out_near[k][0]
        add = (term[:, :half].astype(F32) + from_behind[k].astype(F32)).astype(BF16)
        one.append(move(lax.dynamic_update_slice(term, add, (0, 0)), a, 1))
        term = out_near[2 + k][0]
        add = (term[:, half:].astype(F32) + from_ahead[k].astype(F32)).astype(BF16)
        two.append(move(lax.dynamic_update_slice(term, add, (0, half)), a, -1))
    one, two = hold((one, two))
    summed = []
    for k, a in enumerate(firsts):
        four = (out_own[k][0].astype(F32) + one[k].astype(F32) + two[k].astype(F32)).astype(BF16)
        n = four.shape[0] // SIDE
        summed.append(scatter_direct([four[i * n : (i + 1) * n] for i in range(SIDE)], a).astype(BF16))
    back = lax.all_to_all(
        jnp.concatenate(summed, axis=0).reshape(nodes, CAPACITY, features),
        "node",
        split_axis=0,
        concat_axis=0,
        tiled=True,
    ).reshape(routed, features)
    return jnp.dot(pick[:, :routed].astype(BF16), back, preferred_element_type=F32).astype(BF16)


def solution(mesh):
    placed = (
        P(("node", "local"), None),
        P(("node", "local"), None),
        P(("node", "local"), None),
        P(),
        P("node", None, "local"),
        P("node", None, "local"),
        P("node", "local", None),
        P(None, "local"),
        P(None, "local"),
        P("local", None),
    )
    return jax.shard_map(
        per_device, mesh=mesh, in_specs=placed, out_specs=P(("node", "local"), None), check_vma=False
    )
```

```python
import jax
import jax.numpy as jnp
from jax import lax
from jax.experimental import pallas as pl
from jax.experimental.pallas import tpu as pltpu
from jax.sharding import PartitionSpec as P

SIDE = 4
NODES, CORES = 16, 2
CAPACITY = 2
AUX = 128
BF16, F32 = jnp.bfloat16, jnp.float32


def move(value, phase, step):
    pairs = []
    for node in range(NODES):
        for y in range(SIDE):
            for x in range(SIDE):
                if node % CORES == phase:
                    ty, tx = y, (x + step) % SIDE
                else:
                    ty, tx = (y + step) % SIDE, x
                base = node * SIDE * SIDE
                pairs.append((base + y * SIDE + x, base + ty * SIDE + tx))
    return lax.ppermute(value, ("node", "local"), pairs)


def gather_direct(block, phase):
    return [block, move(block, phase, -1), move(block, phase, 1), move(block, phase, 2)]


def scatter_direct(terms, phase):
    got = [move(terms[1], phase, 1), move(terms[2], phase, -1), move(terms[3], phase, 2)]
    return sum((g.astype(F32) for g in got), terms[0].astype(F32))


def call(kernel, outs, scratch, cost, *args):
    return pl.pallas_call(
        kernel,
        out_shape=outs,
        in_specs=[pl.BlockSpec(memory_space=pltpu.VMEM)] * len(args),
        out_specs=[pl.BlockSpec(memory_space=pltpu.VMEM)] * len(outs),
        scratch_shapes=scratch,
        compiler_params=pltpu.CompilerParams(vmem_limit_bytes=28 * 1024 * 1024),
        cost_estimate=cost,
    )(*args)


def dispatch_kernel(ids, scales, placement, tokens, blocks, pick):
    own, features = tokens.shape
    nodes, routed = placement.shape[1], blocks.shape[0]

    def iota(shape, axis):
        return lax.broadcasted_iota(jnp.int32, shape, axis)

    square = (nodes, nodes)
    place = jnp.sum(jnp.where(iota(square, 0) == iota(square, 1), placement[...], 0), axis=1, keepdims=True)
    label = iota((nodes, own), 0)
    hits, counts = [], jnp.zeros((nodes, own), F32)
    for k in range(ids.shape[0]):
        target = jnp.sum(jnp.where(ids[k : k + 1, :] == label, place, 0), axis=0, keepdims=True)
        hits.append((target, jnp.where(target == label, 1.0, 0.0)))
        counts += hits[-1][1]
    before = jnp.where(iota((own, own), 0) < iota((own, own), 1), 1.0, 0.0)
    earlier = jnp.dot(counts, before, preferred_element_type=F32)
    row = iota((routed, own), 0)
    table, scale = jnp.zeros((routed, own), F32), jnp.zeros((routed, 1), F32)
    for k, (target, hit) in enumerate(hits):
        position = jnp.sum(earlier * hit, axis=0, keepdims=True).astype(jnp.int32)
        mark = jnp.where(target * CAPACITY + position == row, 1.0, 0.0)
        table += mark
        scale += jnp.sum(mark * scales[k : k + 1, :], axis=1, keepdims=True)
        if k == 0:
            flag = jnp.sum(mark, axis=1, keepdims=True)
    high = scale.astype(BF16).astype(F32)
    middle = (scale - high).astype(BF16).astype(F32)
    low = scale - high - middle
    column = iota((routed, AUX), 1)
    aux = jnp.where(column == 0, high, jnp.where(column == 1, middle, jnp.where(column == 2, low, 0.0)))
    aux = jnp.where(column == 3, flag, aux)
    pick[...] = table
    blocks[:, 0:features] = jnp.dot(table.astype(BF16), tokens[...], preferred_element_type=F32).astype(BF16)
    blocks[:, features : features + AUX] = aux.astype(BF16)


def dispatch(ids, scales, placement, tokens):
    own, features = tokens.shape
    routed = placement.shape[0] * CAPACITY
    return call(
        dispatch_kernel,
        [jax.ShapeDtypeStruct((routed, features + AUX), BF16), jax.ShapeDtypeStruct((routed, own), F32)],
        [],
        pl.CostEstimate(flops=2 * own * routed * features, bytes_accessed=4 * routed * features, transcendentals=0),
        ids.T,
        scales.T,
        placement.reshape(1, -1),
        tokens,
    )


def mlp_kernel(pieces, *refs):
    count = sum(pieces)
    ins, weights, outs = refs[:count], refs[count : count + 6], refs[count + 6 : 2 * count + 6]
    acc = refs[2 * count + 6]
    gate, up, down, shared_gate, shared_up, shared_down = weights
    features, width = gate.shape
    places, at = [], 0
    for parts in pieces:
        places.append(range(at, at + parts))
        at += parts
    rows = [ins[p[0]].shape[0] for p in places]

    def read(base, size):
        values = []
        for p in places:
            first = outs[p[0]].shape[1]
            which = min(base // first, len(p) - 1)
            values.append(ins[p[which]][:, pl.ds(base - which * first, size)])
        return jnp.concatenate(values, axis=0)

    chunk = 1792
    for base in range(0, features, chunk):
        x = read(base, chunk)
        for k, (one, two) in enumerate(((gate, up), (shared_gate, shared_up))):
            weight = jnp.concatenate([one[pl.ds(base, chunk), :], two[pl.ds(base, chunk), :]], axis=1)
            got = jnp.dot(x, weight, preferred_element_type=F32)
            acc[k] = got if base == 0 else acc[k] + got
    aux = read(features, AUX).astype(F32)
    factors = (aux[:, 0:1] + aux[:, 1:2] + aux[:, 2:3], aux[:, 3:4])
    hidden = []
    for k, factor in enumerate(factors):
        g = acc[k, :, :width]
        hidden.append((g / (1.0 + jnp.exp(-g)) * acc[k, :, width:] * factor).astype(BF16))
    hidden = jnp.concatenate(hidden, axis=1)

    step = 512
    shortest = min(o.shape[1] for o in outs)

    for start in range(0, features, shortest):

        @pl.loop(0, shortest // step)
        def _(c):
            at = pl.multiple_of(c * step, step)
            columns = pl.ds(start + at, step)
            weight = jnp.concatenate([down[:, columns], shared_down[:, columns]], axis=0)
            got = jnp.dot(hidden, weight, preferred_element_type=F32).astype(BF16)
            first = 0
            for p, n in zip(places, rows, strict=True):
                size = outs[p[0]].shape[1]
                outs[p[start // size]][:, pl.ds(start % size + at, step)] = got[first : first + n]
                first += n


def mlp(pieces, weights):
    flat = [a for p in pieces for a in p]
    counts = [len(p) for p in pieces]
    rows = sum(p[0].shape[0] for p in pieces)
    features, width = weights[0].shape
    outs = call(
        lambda *refs: mlp_kernel(counts, *refs),
        [jax.ShapeDtypeStruct((p[0].shape[0], features // len(p)), BF16) for p in pieces for _ in p],
        [pltpu.VMEM((2, rows, 2 * width), F32)],
        pl.CostEstimate(
            flops=2 * 6 * rows * features * width,
            bytes_accessed=2 * (2 * rows * features + 6 * features * width),
            transcendentals=2 * rows * width,
        ),
        *flat,
        *weights,
    )
    split, at = [], 0
    for n in counts:
        split.append(outs[at : at + n])
        at += n
    return split


def per_device(
    tokens, expert_ids, gate_scales, placement, expert_gate, expert_up, expert_down, shared_gate, shared_up, shared_down
):
    nodes = lax.axis_size("node")
    features = tokens.shape[1]
    routed = nodes * CAPACITY
    half = features // 2
    weights = (expert_gate[0], expert_up[0], expert_down[0], shared_gate, shared_up, shared_down)
    hold = lax.optimization_barrier

    blocks, pick = dispatch(expert_ids, gate_scales, placement, tokens)
    arrived = lax.all_to_all(
        blocks.reshape(nodes, CAPACITY, -1), "node", split_axis=0, concat_axis=0, tiled=True
    ).reshape(routed, -1)

    size = routed // 2
    near = [jnp.concatenate(gather_direct(arrived[h * size : (h + 1) * size], 0), axis=0) for h in range(2)]
    ahead, behind = [move(n, 1, -1) for n in near], [move(n, 1, 1) for n in near]
    out_own = mlp([[n] for n in near], weights)
    ahead[0], behind[0], out_own = hold((ahead[0], behind[0], out_own))
    left = [move(v[:, :half], 1, -1) for v in ahead]
    right = [move(v[:, half:], 1, 1) for v in behind]
    out_near = [mlp([[ahead[0]], [behind[0]]], weights)]
    left[0], right[0], out_near = hold((left[0], right[0], out_near))
    out_far = [mlp([[p, q]], weights)[0] for p, q in zip(left, right, strict=True)]
    ahead[1], behind[1], out_far[1] = hold((ahead[1], behind[1], out_far[1]))
    out_near.append(mlp([[ahead[1]], [behind[1]]], weights))

    summed = []
    for h in range(2):
        from_behind, from_ahead = move(out_far[h][0], 1, 1), move(out_far[h][1], 1, -1)
        (out_ahead,), (out_behind,) = out_near[h]
        add = (out_ahead[:, :half].astype(F32) + from_behind.astype(F32)).astype(BF16)
        one = move(lax.dynamic_update_slice(out_ahead, add, (0, 0)), 1, 1)
        add = (out_behind[:, half:].astype(F32) + from_ahead.astype(F32)).astype(BF16)
        two = move(lax.dynamic_update_slice(out_behind, add, (0, half)), 1, -1)
        four = (out_own[h][0].astype(F32) + one.astype(F32) + two.astype(F32)).astype(BF16)
        summed.append(scatter_direct([four[i * size : (i + 1) * size] for i in range(SIDE)], 0).astype(BF16))
    summed = jnp.concatenate(summed, axis=0)
    back = lax.all_to_all(
        summed.reshape(nodes, CAPACITY, features), "node", split_axis=0, concat_axis=0, tiled=True
    ).reshape(routed, features)
    return lax.dot_general(
        pick.astype(BF16), back, (((0,), (0,)), ((), ())), preferred_element_type=F32
    ).astype(BF16)


def solution(mesh):
    placed = (
        P(("node", "local"), None),
        P(("node", "local"), None),
        P(("node", "local"), None),
        P(),
        P("node", None, "local"),
        P("node", None, "local"),
        P("node", "local", None),
        P(None, "local"),
        P(None, "local"),
        P("local", None),
    )
    return jax.shard_map(
        per_device, mesh=mesh, in_specs=placed, out_specs=P(("node", "local"), None), check_vma=False
    )
```

```python
import jax
import jax.numpy as jnp
from jax import lax
from jax.experimental import pallas as pl
from jax.experimental.pallas import tpu as pltpu
from jax.sharding import PartitionSpec as P

SIDE = 4
NODES, CORES = 16, 2
CAPACITY = 2
AUX = 128
BF16, F32 = jnp.bfloat16, jnp.float32


def move(value, phase, step):
    pairs = []
    for node in range(NODES):
        for y in range(SIDE):
            for x in range(SIDE):
                if node % CORES == phase:
                    ty, tx = y, (x + step) % SIDE
                else:
                    ty, tx = (y + step) % SIDE, x
                base = node * SIDE * SIDE
                pairs.append((base + y * SIDE + x, base + ty * SIDE + tx))
    return lax.ppermute(value, ("node", "local"), pairs)


def gather_direct(block, phase):
    return [block, move(block, phase, -1), move(block, phase, 1), move(block, phase, 2)]


def scatter_direct(terms, phase):
    got = [move(terms[1], phase, 1), move(terms[2], phase, -1), move(terms[3], phase, 2)]
    return sum((g.astype(F32) for g in got), terms[0].astype(F32))


def call(kernel, outs, scratch, cost, *args):
    return pl.pallas_call(
        kernel,
        out_shape=outs,
        in_specs=[pl.BlockSpec(memory_space=pltpu.VMEM)] * len(args),
        out_specs=[pl.BlockSpec(memory_space=pltpu.VMEM)] * len(outs),
        scratch_shapes=scratch,
        compiler_params=pltpu.CompilerParams(vmem_limit_bytes=28 * 1024 * 1024),
        cost_estimate=cost,
    )(*args)


def dispatch_kernel(ids, scales, placement, tokens, blocks, pick):
    own, features = tokens.shape
    nodes, routed = placement.shape[1], blocks.shape[0]

    def iota(shape, axis):
        return lax.broadcasted_iota(jnp.int32, shape, axis)

    square = (nodes, nodes)
    place = jnp.sum(jnp.where(iota(square, 0) == iota(square, 1), placement[...], 0), axis=1, keepdims=True)
    label = iota((nodes, own), 0)
    hits, counts = [], jnp.zeros((nodes, own), F32)
    for k in range(ids.shape[0]):
        target = jnp.sum(jnp.where(ids[k : k + 1, :] == label, place, 0), axis=0, keepdims=True)
        hits.append((target, jnp.where(target == label, 1.0, 0.0)))
        counts += hits[-1][1]
    before = jnp.where(iota((own, own), 0) < iota((own, own), 1), 1.0, 0.0)
    earlier = jnp.dot(counts, before, preferred_element_type=F32)
    row = iota((routed, own), 0)
    table, scale = jnp.zeros((routed, own), F32), jnp.zeros((routed, 1), F32)
    for k, (target, hit) in enumerate(hits):
        position = jnp.sum(earlier * hit, axis=0, keepdims=True).astype(jnp.int32)
        mark = jnp.where(target * CAPACITY + position == row, 1.0, 0.0)
        table += mark
        scale += jnp.sum(mark * scales[k : k + 1, :], axis=1, keepdims=True)
        if k == 0:
            flag = jnp.sum(mark, axis=1, keepdims=True)
    high = scale.astype(BF16).astype(F32)
    middle = (scale - high).astype(BF16).astype(F32)
    low = scale - high - middle
    column = iota((routed, AUX), 1)
    aux = jnp.where(column == 0, high, jnp.where(column == 1, middle, jnp.where(column == 2, low, 0.0)))
    aux = jnp.where(column == 3, flag, aux)
    pick[...] = table
    blocks[:, 0:features] = jnp.dot(table.astype(BF16), tokens[...], preferred_element_type=F32).astype(BF16)
    blocks[:, features : features + AUX] = aux.astype(BF16)


def dispatch(ids, scales, placement, tokens):
    own, features = tokens.shape
    routed = placement.shape[0] * CAPACITY
    return call(
        dispatch_kernel,
        [jax.ShapeDtypeStruct((routed, features + AUX), BF16), jax.ShapeDtypeStruct((routed, own), F32)],
        [],
        pl.CostEstimate(flops=2 * own * routed * features, bytes_accessed=4 * routed * features, transcendentals=0),
        ids.T,
        scales.T,
        placement.reshape(1, -1),
        tokens,
    )


def mlp_kernel(pieces, *refs):
    count = sum(pieces)
    ins, weights, outs = refs[:count], refs[count : count + 6], refs[count + 6 : 2 * count + 6]
    acc = refs[2 * count + 6]
    gate, up, down, shared_gate, shared_up, shared_down = weights
    features, width = gate.shape
    places, at = [], 0
    for parts in pieces:
        places.append(range(at, at + parts))
        at += parts
    rows = [ins[p[0]].shape[0] for p in places]

    def read(base, size):
        values = []
        for p in places:
            first = outs[p[0]].shape[1]
            which = min(base // first, len(p) - 1)
            values.append(ins[p[which]][:, pl.ds(base - which * first, size)])
        return jnp.concatenate(values, axis=0)

    chunk = 1792
    for base in range(0, features, chunk):
        x = read(base, chunk)
        for k, (one, two) in enumerate(((gate, up), (shared_gate, shared_up))):
            weight = jnp.concatenate([one[pl.ds(base, chunk), :], two[pl.ds(base, chunk), :]], axis=1)
            got = jnp.dot(x, weight, preferred_element_type=F32)
            acc[k] = got if base == 0 else acc[k] + got
    aux = read(features, AUX).astype(F32)
    factors = (aux[:, 0:1] + aux[:, 1:2] + aux[:, 2:3], aux[:, 3:4])
    hidden = []
    for k, factor in enumerate(factors):
        g = acc[k, :, :width]
        hidden.append((g / (1.0 + jnp.exp(-g)) * acc[k, :, width:] * factor).astype(BF16))
    hidden = jnp.concatenate(hidden, axis=1)

    step = 512
    shortest = min(o.shape[1] for o in outs)

    for start in range(0, features, shortest):

        @pl.loop(0, shortest // step)
        def _(c):
            at = pl.multiple_of(c * step, step)
            columns = pl.ds(start + at, step)
            weight = jnp.concatenate([down[:, columns], shared_down[:, columns]], axis=0)
            got = jnp.dot(hidden, weight, preferred_element_type=F32).astype(BF16)
            first = 0
            for p, n in zip(places, rows, strict=True):
                size = outs[p[0]].shape[1]
                outs[p[start // size]][:, pl.ds(start % size + at, step)] = got[first : first + n]
                first += n


def mlp(pieces, weights):
    flat = [a for p in pieces for a in p]
    counts = [len(p) for p in pieces]
    rows = sum(p[0].shape[0] for p in pieces)
    features, width = weights[0].shape
    outs = call(
        lambda *refs: mlp_kernel(counts, *refs),
        [jax.ShapeDtypeStruct((p[0].shape[0], features // len(p)), BF16) for p in pieces for _ in p],
        [pltpu.VMEM((2, rows, 2 * width), F32)],
        pl.CostEstimate(
            flops=2 * 6 * rows * features * width,
            bytes_accessed=2 * (2 * rows * features + 6 * features * width),
            transcendentals=2 * rows * width,
        ),
        *flat,
        *weights,
    )
    split, at = [], 0
    for n in counts:
        split.append(outs[at : at + n])
        at += n
    return split


def per_device(
    tokens, expert_ids, gate_scales, placement, expert_gate, expert_up, expert_down, shared_gate, shared_up, shared_down
):
    nodes = lax.axis_size("node")
    features = tokens.shape[1]
    routed = nodes * CAPACITY
    half = features // 2
    weights = (expert_gate[0], expert_up[0], expert_down[0], shared_gate, shared_up, shared_down)
    hold = lax.optimization_barrier

    blocks, pick = dispatch(expert_ids, gate_scales, placement, tokens)
    arrived = lax.all_to_all(
        blocks.reshape(nodes, CAPACITY, -1), "node", split_axis=0, concat_axis=0, tiled=True
    ).reshape(routed, -1)

    size = routed // 2
    near = [jnp.concatenate(gather_direct(arrived[h * size : (h + 1) * size], 0), axis=0) for h in range(2)]
    ahead, behind = [move(n, 1, -1) for n in near], [move(n, 1, 1) for n in near]
    out_own = mlp([[n] for n in near], weights)
    ahead[0], behind[0], out_own = hold((ahead[0], behind[0], out_own))
    out_near = [mlp([[ahead[0]], [behind[0]]], weights)]
    ahead[1], behind[1], out_near = hold((ahead[1], behind[1], out_near))
    left = [move(v[:, :half], 1, -1) for v in ahead]
    right = [move(v[:, half:], 1, 1) for v in behind]
    out_far = [mlp([[p, q]], weights)[0] for p, q in zip(left, right, strict=True)]
    ahead[1], behind[1], out_far[1] = hold((ahead[1], behind[1], out_far[1]))
    out_near.append(mlp([[ahead[1]], [behind[1]]], weights))

    summed = []
    for h in range(2):
        from_behind, from_ahead = move(out_far[h][0], 1, 1), move(out_far[h][1], 1, -1)
        (out_ahead,), (out_behind,) = out_near[h]
        add = (out_ahead[:, :half].astype(F32) + from_behind.astype(F32)).astype(BF16)
        one = move(lax.dynamic_update_slice(out_ahead, add, (0, 0)), 1, 1)
        add = (out_behind[:, half:].astype(F32) + from_ahead.astype(F32)).astype(BF16)
        two = move(lax.dynamic_update_slice(out_behind, add, (0, half)), 1, -1)
        four = (out_own[h][0].astype(F32) + one.astype(F32) + two.astype(F32)).astype(BF16)
        summed.append(scatter_direct([four[i * size : (i + 1) * size] for i in range(SIDE)], 0).astype(BF16))
    summed = jnp.concatenate(summed, axis=0)
    back = lax.all_to_all(
        summed.reshape(nodes, CAPACITY, features), "node", split_axis=0, concat_axis=0, tiled=True
    ).reshape(routed, features)
    return lax.dot_general(
        pick.astype(BF16), back, (((0,), (0,)), ((), ())), preferred_element_type=F32
    ).astype(BF16)


def solution(mesh):
    placed = (
        P(("node", "local"), None),
        P(("node", "local"), None),
        P(("node", "local"), None),
        P(),
        P("node", None, "local"),
        P("node", None, "local"),
        P("node", "local", None),
        P(None, "local"),
        P(None, "local"),
        P("local", None),
    )
    return jax.shard_map(
        per_device, mesh=mesh, in_specs=placed, out_specs=P(("node", "local"), None), check_vma=False
    )
```

```python
import jax
import jax.numpy as jnp
from jax import lax
from jax.experimental import pallas as pl
from jax.experimental.pallas import tpu as pltpu
from jax.sharding import PartitionSpec as P

SIDE = 4
NODES, CORES = 16, 2
CAPACITY = 2
AUX = 128
BF16, F32 = jnp.bfloat16, jnp.float32


def move(value, phase, step):
    pairs = []
    for node in range(NODES):
        for y in range(SIDE):
            for x in range(SIDE):
                if node % CORES == phase:
                    ty, tx = y, (x + step) % SIDE
                else:
                    ty, tx = (y + step) % SIDE, x
                base = node * SIDE * SIDE
                pairs.append((base + y * SIDE + x, base + ty * SIDE + tx))
    return lax.ppermute(value, ("node", "local"), pairs)


def gather_direct(block, phase):
    return [block, move(block, phase, -1), move(block, phase, 1), move(block, phase, 2)]


def scatter_direct(terms, phase):
    got = [move(terms[1], phase, 1), move(terms[2], phase, -1), move(terms[3], phase, 2)]
    return sum((g.astype(F32) for g in got), terms[0].astype(F32))


def call(kernel, outs, scratch, cost, *args):
    return pl.pallas_call(
        kernel,
        out_shape=outs,
        in_specs=[pl.BlockSpec(memory_space=pltpu.VMEM)] * len(args),
        out_specs=[pl.BlockSpec(memory_space=pltpu.VMEM)] * len(outs),
        scratch_shapes=scratch,
        compiler_params=pltpu.CompilerParams(vmem_limit_bytes=28 * 1024 * 1024),
        cost_estimate=cost,
    )(*args)


def dispatch_kernel(ids, scales, placement, tokens, blocks, pick):
    own, features = tokens.shape
    nodes, routed = placement.shape[1], blocks.shape[0]

    def iota(shape, axis):
        return lax.broadcasted_iota(jnp.int32, shape, axis)

    square = (nodes, nodes)
    place = jnp.sum(jnp.where(iota(square, 0) == iota(square, 1), placement[...], 0), axis=1, keepdims=True)
    label = iota((nodes, own), 0)
    hits, counts = [], jnp.zeros((nodes, own), F32)
    for k in range(ids.shape[0]):
        target = jnp.sum(jnp.where(ids[k : k + 1, :] == label, place, 0), axis=0, keepdims=True)
        hits.append((target, jnp.where(target == label, 1.0, 0.0)))
        counts += hits[-1][1]
    before = jnp.where(iota((own, own), 0) < iota((own, own), 1), 1.0, 0.0)
    earlier = jnp.dot(counts, before, preferred_element_type=F32)
    row = iota((routed, own), 0)
    table, scale = jnp.zeros((routed, own), F32), jnp.zeros((routed, 1), F32)
    for k, (target, hit) in enumerate(hits):
        position = jnp.sum(earlier * hit, axis=0, keepdims=True).astype(jnp.int32)
        mark = jnp.where(target * CAPACITY + position == row, 1.0, 0.0)
        table += mark
        scale += jnp.sum(mark * scales[k : k + 1, :], axis=1, keepdims=True)
        if k == 0:
            flag = jnp.sum(mark, axis=1, keepdims=True)
    high = scale.astype(BF16).astype(F32)
    middle = (scale - high).astype(BF16).astype(F32)
    low = scale - high - middle
    column = iota((routed, AUX), 1)
    aux = jnp.where(column == 0, high, jnp.where(column == 1, middle, jnp.where(column == 2, low, 0.0)))
    aux = jnp.where(column == 3, flag, aux)
    pick[...] = table
    blocks[:, 0:features] = jnp.dot(table.astype(BF16), tokens[...], preferred_element_type=F32).astype(BF16)
    blocks[:, features : features + AUX] = aux.astype(BF16)


def dispatch(ids, scales, placement, tokens):
    own, features = tokens.shape
    routed = placement.shape[0] * CAPACITY
    return call(
        dispatch_kernel,
        [jax.ShapeDtypeStruct((routed, features + AUX), BF16), jax.ShapeDtypeStruct((routed, own), F32)],
        [],
        pl.CostEstimate(flops=2 * own * routed * features, bytes_accessed=4 * routed * features, transcendentals=0),
        ids.T,
        scales.T,
        placement.reshape(1, -1),
        tokens,
    )


def mlp_kernel(pieces, *refs):
    count = sum(pieces)
    ins, weights, outs = refs[:count], refs[count : count + 6], refs[count + 6 : 2 * count + 6]
    acc = refs[2 * count + 6]
    gate, up, down, shared_gate, shared_up, shared_down = weights
    features, width = gate.shape
    places, at = [], 0
    for parts in pieces:
        places.append(range(at, at + parts))
        at += parts
    rows = [ins[p[0]].shape[0] for p in places]

    def read(base, size):
        values = []
        for p in places:
            first = outs[p[0]].shape[1]
            which = min(base // first, len(p) - 1)
            values.append(ins[p[which]][:, pl.ds(base - which * first, size)])
        return jnp.concatenate(values, axis=0)

    chunk = 1792
    for base in range(0, features, chunk):
        x = read(base, chunk)
        for k, (one, two) in enumerate(((gate, up), (shared_gate, shared_up))):
            weight = jnp.concatenate([one[pl.ds(base, chunk), :], two[pl.ds(base, chunk), :]], axis=1)
            got = jnp.dot(x, weight, preferred_element_type=F32)
            acc[k] = got if base == 0 else acc[k] + got
    aux = read(features, AUX).astype(F32)
    factors = (aux[:, 0:1] + aux[:, 1:2] + aux[:, 2:3], aux[:, 3:4])
    hidden = []
    for k, factor in enumerate(factors):
        g = acc[k, :, :width]
        hidden.append((g / (1.0 + jnp.exp(-g)) * acc[k, :, width:] * factor).astype(BF16))
    hidden = jnp.concatenate(hidden, axis=1)

    step = 512
    shortest = min(o.shape[1] for o in outs)

    for start in range(0, features, shortest):

        @pl.loop(0, shortest // step, unroll=True)
        def _(c):
            at = pl.multiple_of(c * step, step)
            columns = pl.ds(start + at, step)
            weight = jnp.concatenate([down[:, columns], shared_down[:, columns]], axis=0)
            got = jnp.dot(hidden, weight, preferred_element_type=F32).astype(BF16)
            first = 0
            for p, n in zip(places, rows, strict=True):
                size = outs[p[0]].shape[1]
                outs[p[start // size]][:, pl.ds(start % size + at, step)] = got[first : first + n]
                first += n


def mlp(pieces, weights):
    flat = [a for p in pieces for a in p]
    counts = [len(p) for p in pieces]
    rows = sum(p[0].shape[0] for p in pieces)
    features, width = weights[0].shape
    outs = call(
        lambda *refs: mlp_kernel(counts, *refs),
        [jax.ShapeDtypeStruct((p[0].shape[0], features // len(p)), BF16) for p in pieces for _ in p],
        [pltpu.VMEM((2, rows, 2 * width), F32)],
        pl.CostEstimate(
            flops=2 * 6 * rows * features * width,
            bytes_accessed=2 * (2 * rows * features + 6 * features * width),
            transcendentals=2 * rows * width,
        ),
        *flat,
        *weights,
    )
    split, at = [], 0
    for n in counts:
        split.append(outs[at : at + n])
        at += n
    return split


def per_device(
    tokens, expert_ids, gate_scales, placement, expert_gate, expert_up, expert_down, shared_gate, shared_up, shared_down
):
    nodes = lax.axis_size("node")
    features = tokens.shape[1]
    routed = nodes * CAPACITY
    half = features // 2
    weights = (expert_gate[0], expert_up[0], expert_down[0], shared_gate, shared_up, shared_down)
    hold = lax.optimization_barrier

    blocks, pick = dispatch(expert_ids, gate_scales, placement, tokens)
    arrived = lax.all_to_all(
        blocks.reshape(nodes, CAPACITY, -1), "node", split_axis=0, concat_axis=0, tiled=True
    ).reshape(routed, -1)

    size = routed // 2
    near = [jnp.concatenate(gather_direct(arrived[h * size : (h + 1) * size], 0), axis=0) for h in range(2)]
    ahead, behind = [move(n, 1, -1) for n in near], [move(n, 1, 1) for n in near]
    out_own = mlp([[n] for n in near], weights)
    ahead[0], behind[0], out_own = hold((ahead[0], behind[0], out_own))
    out_near = [mlp([[ahead[0]], [behind[0]]], weights)]
    ahead[1], behind[1], out_near = hold((ahead[1], behind[1], out_near))
    left = [move(v[:, :half], 1, -1) for v in ahead]
    right = [move(v[:, half:], 1, 1) for v in behind]
    out_far = [mlp([[p, q]], weights)[0] for p, q in zip(left, right, strict=True)]
    ahead[1], behind[1], out_far[1] = hold((ahead[1], behind[1], out_far[1]))
    out_near.append(mlp([[ahead[1]], [behind[1]]], weights))

    summed = []
    for h in range(2):
        from_behind, from_ahead = move(out_far[h][0], 1, 1), move(out_far[h][1], 1, -1)
        (out_ahead,), (out_behind,) = out_near[h]
        add = (out_ahead[:, :half].astype(F32) + from_behind.astype(F32)).astype(BF16)
        one = move(lax.dynamic_update_slice(out_ahead, add, (0, 0)), 1, 1)
        add = (out_behind[:, half:].astype(F32) + from_ahead.astype(F32)).astype(BF16)
        two = move(lax.dynamic_update_slice(out_behind, add, (0, half)), 1, -1)
        four = (out_own[h][0].astype(F32) + one.astype(F32) + two.astype(F32)).astype(BF16)
        summed.append(scatter_direct([four[i * size : (i + 1) * size] for i in range(SIDE)], 0).astype(BF16))
    summed = jnp.concatenate(summed, axis=0)
    back = lax.all_to_all(
        summed.reshape(nodes, CAPACITY, features), "node", split_axis=0, concat_axis=0, tiled=True
    ).reshape(routed, features)
    return lax.dot_general(
        pick.astype(BF16), back, (((0,), (0,)), ((), ())), preferred_element_type=F32
    ).astype(BF16)


def solution(mesh):
    placed = (
        P(("node", "local"), None),
        P(("node", "local"), None),
        P(("node", "local"), None),
        P(),
        P("node", None, "local"),
        P("node", None, "local"),
        P("node", "local", None),
        P(None, "local"),
        P(None, "local"),
        P("local", None),
    )
    return jax.shard_map(
        per_device, mesh=mesh, in_specs=placed, out_specs=P(("node", "local"), None), check_vma=False
    )
```
